32 devices in a mesh: bx: 4 (over z), by: 8 (over y, x, core).
Axes of the slice: x: 2, y: 2, z: 4, core: 2. Of those that a mesh axis runs over, the one named last changes fastest.
Arguments:
- rhs: float32 [8, 16, 256, 384], P('bx', 'by'), may hold values from -6 to 6
- perm1: int32 [8, 16, 256], P('bx', 'by'), may hold values from 0 to 255, each once within a row
- interp1: bfloat16 [8, 16, 160, 96], P('bx', 'by'), may hold values from -0.5 to 0.5
- pivinv1: bfloat16 [8, 16, 160, 160], P('bx', 'by'), may hold values from -0.5 to 0.5
- couple1: bfloat16 [8, 16, 8, 96, 160], P('bx', 'by'), may hold values from -0.15625 to 0.15625
- perm2: int32 [4, 8, 384], P('bx', 'by'), may hold values from 0 to 383, each once within a row
- interp2: bfloat16 [4, 8, 256, 128], P('bx', 'by'), may hold values from -0.375 to 0.375
- pivinv2: bfloat16 [4, 8, 256, 256], P('bx', 'by'), may hold values from -0.375 to 0.375
- couple2: bfloat16 [4, 8, 8, 128, 256], P('bx', 'by'), may hold values from -0.125 to 0.125
Outputs:
- red1: bfloat16 [8, 16, 160, 384], P('bx', 'by')
- red2: bfloat16 [4, 8, 256, 384], P('bx', 'by')
- skel2: float32 [4, 8, 128, 384], P('bx', 'by')
The draws below stay inside these ranges and needn't reach their ends.
Inputs may be any that keep to these rules, and one draw needn't show every extreme that they name: Each row of perm1 holds every point index once. Each row of perm2 holds every point index once.
All inputs are finite; a program needn't handle non-finite values.
Results may differ from the reference program's by a relative error of at most 0.013.
Values may be sent and summed in bfloat16 or wider, within the bound.
A program may use at most 64 MiB of HBM per device.

```python
import jax
import jax.numpy as jnp
from jax import lax

S1 = 96
R1 = 160
S2 = 128
K = 384
P1 = 256
P2 = 384
R2 = 256
NBX = 8
NBY = 16
NPX = 4
NPY = 8


def levels(stream_key, dims, cuts, low, top_value):
    gain, own = 1.0, jax.random.fold_in(stream_key, 6)
    for axis_at, parts in cuts:
        heights = jnp.exp(jax.random.uniform(jax.random.fold_in(own, axis_at), (parts,), jnp.float32, low / len(cuts), top_value / len(cuts)))
        gain = gain * jnp.repeat(heights, dims[axis_at] // parts).reshape([-1 if axis == axis_at else 1 for axis in range(len(dims))])
    return gain


def noise(rng, dims, spread, limit, cuts=(), kind=jnp.bfloat16):
    gain = levels(rng, dims, cuts, -0.22, 0.18) if cuts else 1.0
    array = jax.random.normal(rng, dims, jnp.float32) * spread * gain
    return jnp.minimum(jnp.maximum(array, -limit), limit).astype(kind)


def setup_inputs(seed: int = 0) -> dict:
    key_list = jax.random.split(jax.random.key(seed), 10)
    return {
        "rhs": noise(key_list[0], (NBX, NBY, P1, K), 1.0, 6.0, ((0, 4), (1, 8)), jnp.float32),
        "perm1": jax.vmap(lambda own: jax.random.permutation(own, P1))(jax.random.split(key_list[1], NBX * NBY)).reshape((NBX, NBY, P1)).astype(jnp.int32),
        "interp1": noise(key_list[2], (NBX, NBY, R1, S1), R1 ** -0.5, 0.5, ((0, 4), (1, 8))),
        "pivinv1": noise(key_list[3], (NBX, NBY, R1, R1), R1 ** -0.5, 0.5, ((0, 4), (1, 8))),
        "couple1": noise(key_list[4], (NBX, NBY, 8, S1, R1), (8 * R1) ** -0.5, 0.15625, ((0, 4), (1, 8))),
        "perm2": jax.vmap(lambda own: jax.random.permutation(own, P2))(jax.random.split(key_list[5], NPX * NPY)).reshape((NPX, NPY, P2)).astype(jnp.int32),
        "interp2": noise(key_list[6], (NPX, NPY, R2, S2), R2 ** -0.5, 0.375, ((0, 4), (1, 8))),
        "pivinv2": noise(key_list[7], (NPX, NPY, R2, R2), R2 ** -0.5, 0.375, ((0, 4), (1, 8))),
        "couple2": noise(key_list[8], (NPX, NPY, 8, S2, R2), (8 * R2) ** -0.5, 0.125, ((0, 4), (1, 8))),
    }


OFFSETS = [(-1, -1), (-1, 0), (-1, 1), (0, -1), (0, 1), (1, -1), (1, 0), (1, 1)]


def rounded(value):
    return lax.optimization_barrier(value.astype(jnp.bfloat16)).astype(jnp.float32)


def eliminate(skel, red, interp, pivinv, couple):
    rows, cols = skel.shape[0], skel.shape[1]
    zall = jnp.zeros(red.shape, jnp.bfloat16)
    for color in range(4):
        a, b = color // 2, color % 2
        skel_c = skel[a::2, b::2]
        tmat = interp[a::2, b::2].astype(jnp.float32)
        diff = red[a::2, b::2] - jnp.einsum('ijrs,ijsk->ijrk', tmat, rounded(skel_c))
        zc = jnp.einsum('ijrq,ijqk->ijrk', pivinv[a::2, b::2].astype(jnp.float32), rounded(diff)).astype(jnp.bfloat16)
        zf = zc.astype(jnp.float32)
        skel = skel.at[a::2, b::2].set(skel_c - jnp.einsum('ijrs,ijrk->ijsk', tmat, zf))
        zall = zall.at[a::2, b::2].set(zc)
        zgrid = jnp.zeros(red.shape, jnp.bfloat16).at[a::2, b::2].set(zc)
        zpad = jnp.pad(zgrid, ((1, 1), (1, 1), (0, 0), (0, 0)))
        for k in range(8):
            dx, dy = OFFSETS[k]
            pa, pb = (a - dx) % 2, (b - dy) % 2
            source = zpad[1 + dx:1 + dx + rows, 1 + dy:1 + dy + cols][pa::2, pb::2].astype(jnp.float32)
            update = jnp.einsum('ijsr,ijrk->ijsk', couple[pa::2, pb::2, k].astype(jnp.float32), source)
            skel = skel.at[pa::2, pb::2].add(-update)
    return skel, zall


def reference(rhs, perm1, interp1, pivinv1, couple1, perm2, interp2, pivinv2, couple2):
    leaf = jnp.take_along_axis(rhs, perm1[:, :, :, None], axis=2)
    skel_leaf, red1 = eliminate(leaf[:, :, :S1], leaf[:, :, S1:], interp1, pivinv1, couple1)
    parents = skel_leaf.reshape(NPX, 2, NPY, 2, S1, K).transpose(0, 2, 1, 3, 4, 5).reshape(NPX, NPY, P2, K)
    parent = jnp.take_along_axis(parents, perm2[:, :, :, None], axis=2)
    skel2, red2 = eliminate(parent[:, :, :S2], parent[:, :, S2:], interp2, pivinv2, couple2)
    return red1, red2, skel2
```

```python
import functools

import jax
import jax.numpy as jnp
from jax import lax
from jax.experimental import pallas as pl
from jax.experimental.pallas import tpu as pltpu
from jax.sharding import PartitionSpec as P

OFFSETS = [(-1, -1), (-1, 0), (-1, 1), (0, -1), (0, 1), (1, -1), (1, 0), (1, 1)]
BF = jnp.bfloat16
F32 = jnp.float32
MESH = pl.DeviceIdType.MESH
OWN, ROW, COL, COR = 0, 1, 2, 3


def dot(a, b):
    return jnp.dot(a, b, preferred_element_type=F32)


def dot_t(a, b):
    return lax.dot_general(a, b, (((0,), (0,)), ((), ())), preferred_element_type=F32)


def sources():
    table = []
    for color in range(4):
        a, b = color // 2, color % 2
        per_box = []
        for box in range(4):
            nx, ny = box // 2, box % 2
            found = []
            if box != color:
                for k, (dx, dy) in enumerate(OFFSETS):
                    r, c = nx + dx, ny + dy
                    if r % 2 == a and c % 2 == b:
                        row_in, col_in = 0 <= r <= 1, 0 <= c <= 1
                        if row_in and col_in:
                            src = OWN
                        elif col_in:
                            src = ROW
                        elif row_in:
                            src = COL
                        else:
                            src = COR
                        found.append((src, k))
            per_box.append(found)
        table.append(per_box)
    return table


TABLE = sources()


def reorder(perm_row, values):
    n = values.shape[0]
    hit = lax.broadcasted_iota(jnp.int32, (n, n), 0) == perm_row
    onehot = jnp.where(hit, 1.0, 0.0).astype(BF)
    high = values.astype(BF)
    low = (values - high.astype(F32)).astype(BF)
    both = dot_t(onehot, jnp.concatenate([high, low], axis=1))
    w = values.shape[1]
    return both[:, :w] + both[:, w:]


def kernel(
    nq, w, s1, s2,
    rhs_h, perm1_h, t1_h, p1_h, c1_h, perm2_h, t2_h, p2_h, c2_h,
    red1_h, red2_h, skel2_h,
    rhs, perm1, t1, p1, c1, perm2, t2, p2, c2,
    skel, red, zb, got, ptop, pred, zp, pgot,
    in_sem, out1_sem, out2_sem, send1, recv1, send2, recv2,
):
    nx, ny = lax.axis_size("bx"), lax.axis_size("by")
    ix, iy = lax.axis_index("bx"), lax.axis_index("by")

    def has(dx, dy):
        cond = None
        for d, i, n in ((dx, ix, nx), (dy, iy, ny)):
            if d:
                here = (i > 0) if d < 0 else (i < n - 1)
                cond = here if cond is None else jnp.logical_and(cond, here)
        return cond

    def load(n, src, dst):
        return pltpu.make_async_copy(src, dst, in_sem.at[n])

    rhs_in = [load(i, rhs_h.at[i // 2, i % 2], rhs.at[i // 2, i % 2]) for i in range(4)]
    rest = [
        load(4 + i, s, d)
        for i, (s, d) in enumerate(
            [(perm1_h, perm1), (t1_h, t1), (p1_h, p1), (c1_h, c1), (perm2_h, perm2), (t2_h, t2), (p2_h, p2), (c2_h, c2)]
        )
    ]
    perm1_in, t1_in, p1_in, c1_in, perm2_in, t2_in, p2_in, c2_in = rest
    for copy in [perm1_in, rhs_in[0], t1_in, p1_in, rhs_in[1], c1_in, rhs_in[2], rhs_in[3], perm2_in, t2_in, p2_in, c2_in]:
        copy.start()

    barrier = pltpu.get_barrier_semaphore()
    sides = [(-1, 0), (1, 0), (0, -1), (0, 1)]
    for dx, dy in sides:
        @pl.when(has(dx, dy))
        def _(dx=dx, dy=dy):
            pl.semaphore_signal(barrier, inc=1, device_id=(ix + dx, iy + dy), device_id_type=MESH)

    for color in range(4):
        sx = 1 if color // 2 else -1
        sy = 1 if color % 2 else -1
        for src, (dx, dy) in ((ROW, (-sx, 0)), (COL, (0, -sy)), (COR, (-sx, -sy))):
            @pl.when(jnp.logical_not(has(dx, dy)))
            def _(color=color, src=src):
                got[color, src - 1] = jnp.zeros(got.shape[2:], BF)
    for k, (dx, dy) in enumerate(OFFSETS):
        @pl.when(jnp.logical_not(has(dx, dy)))
        def _(k=k):
            pgot[k] = jnp.zeros(pgot.shape[1:], BF)

    def unpack(box):
        i, j = box // 2, box % 2
        values = reorder(perm1[i, pl.ds(j, 1), :], rhs[i, j])
        for q in range(nq):
            part = values[:, q * w:(q + 1) * w]
            skel[box, q] = part[:s1]
            red[box, q] = part[s1:]

    perm1_in.wait()
    rhs_in[0].wait()
    unpack(0)
    t1_in.wait()
    p1_in.wait()

    peers = sum(jnp.where(has(dx, dy), 1, 0) for dx, dy in sides)
    pl.semaphore_wait(barrier, peers)

    def leaf_copy(color, src, q):
        sx = 1 if color // 2 else -1
        sy = 1 if color % 2 else -1
        if src == ROW:
            block, to = zb.at[color, q], (ix + sx, iy)
        elif src == COL:
            block, to = zb.at[color, q], (ix, iy + sy)
        else:
            block, to = got.at[color, ROW - 1, q], (ix, iy + sy)
        return pltpu.make_async_remote_copy(
            src_ref=block,
            dst_ref=got.at[color, src - 1, q],
            send_sem=send1.at[color, src - 1, q],
            recv_sem=recv1.at[color, src - 1, q],
            device_id=to,
            device_id_type=MESH,
        )

    def leaf_out(color, src):
        sx = 1 if color // 2 else -1
        sy = 1 if color % 2 else -1
        if src == ROW:
            return has(sx, 0)
        if src == COL:
            return has(0, sy)
        return jnp.logical_and(has(-sx, 0), has(0, sy))

    def leaf_in(color, src):
        sx = 1 if color // 2 else -1
        sy = 1 if color % 2 else -1
        return has(*{ROW: (-sx, 0), COL: (0, -sy), COR: (-sx, -sy)}[src])

    def leaf_send(color, src, q):
        @pl.when(leaf_out(color, src))
        def _():
            leaf_copy(color, src, q).start()

    def leaf_wait(color, src, q):
        @pl.when(leaf_in(color, src))
        def _():
            leaf_copy(color, src, q).wait_recv()

    def leaf_forward(color, q):
        leaf_wait(color, ROW, q)
        leaf_send(color, COR, q)

    def red1_out(color, q):
        a, b = color // 2, color % 2
        return pltpu.make_async_copy(zb.at[color, q], red1_h.at[a, b, :, pl.ds(q * w, w)], out1_sem.at[color, q])

    def solve1(box, q):
        a, b = box // 2, box % 2
        tm = t1[a, b]
        sk = skel[box, q]
        diff = red[box, q] - dot(tm, sk.astype(BF))
        zc = dot(p1[a, b], diff.astype(BF)).astype(BF)
        zb[box, q] = zc
        leaf_send(box, COL, q)
        leaf_send(box, ROW, q)
        red1_out(box, q).start()
        skel[box, q] = sk - dot_t(tm, zc)

    def apply1(box, q, *which):
        total = None
        for color, src in which:
            for s, k in TABLE[color][box]:
                if s == src:
                    z = zb[color, q] if s == OWN else got[color, s - 1, q]
                    term = dot(c1[box // 2, box % 2, k], z)
                    total = term if total is None else total + term
        skel[box, q] = skel[box, q] - total

    qs = range(nq)
    for q in qs:
        solve1(0, q)
    rhs_in[1].wait()
    unpack(1)
    c1_in.wait()
    for q in qs:
        apply1(1, q, (0, OWN))
    for q in qs:
        leaf_wait(0, COL, q)
        apply1(1, q, (0, COL))
        solve1(1, q)
    for box in (2, 3):
        rhs_in[box].wait()
        unpack(box)
    for q in qs:
        leaf_forward(0, q)
    for q in qs:
        apply1(2, q, (0, OWN), (0, ROW), (1, OWN))
    for q in qs:
        leaf_forward(1, q)
    for q in qs:
        leaf_wait(1, COL, q)
        apply1(2, q, (1, ROW), (1, COL))
    for q in qs:
        leaf_wait(1, COR, q)
        apply1(2, q, (1, COR))
        solve1(2, q)
    for q in qs:
        leaf_wait(0, COR, q)
        apply1(3, q, (0, OWN), (0, ROW), (0, COL), (0, COR), (1, OWN), (1, ROW), (2, OWN))
    for q in qs:
        leaf_wait(2, COL, q)
        apply1(3, q, (2, COL))
        solve1(3, q)
    for q in qs:
        leaf_forward(2, q)
    for q in qs:
        apply1(0, q, (1, OWN), (1, COL), (2, OWN), (2, ROW), (3, OWN))
        apply1(1, q, (2, OWN), (2, ROW), (2, COL), (3, OWN))
        apply1(2, q, (3, OWN))
    for q in qs:
        leaf_forward(3, q)
    for q in qs:
        leaf_wait(2, COR, q)
        leaf_wait(3, COL, q)
        apply1(0, q, (3, ROW), (3, COL))
        apply1(1, q, (2, COR), (3, ROW))
        apply1(2, q, (3, COL))

    perm2_in.wait()
    order2 = perm2[0]
    t2_in.wait()
    p2_in.wait()
    c2_in.wait()

    def enter2(q):
        leaf_wait(3, COR, q)
        apply1(0, q, (3, COR))
        children = jnp.concatenate([skel[box, q] for box in range(4)], axis=0)
        values = reorder(order2, children)
        ptop[q] = values[:s2]
        pred[q] = values[s2:]

    slot = {offset: k for k, offset in enumerate(OFFSETS)}

    def parent_copy(n, q):
        if n < 4:
            to = sides[n]
            block, where = zp.at[q], (-to[0], -to[1])
        else:
            dx, dy = sides[(n - 4) // 2][0], sides[2 + n % 2][1]
            to = (0, dy)
            block, where = pgot.at[slot[(dx, 0)], q], (dx, -dy)
        return pltpu.make_async_remote_copy(
            src_ref=block,
            dst_ref=pgot.at[slot[where], q],
            send_sem=send2.at[n, q],
            recv_sem=recv2.at[slot[where], q],
            device_id=(ix + to[0], iy + to[1]),
            device_id_type=MESH,
        )

    def parent_out(n):
        if n < 4:
            return has(*sides[n])
        return has(sides[(n - 4) // 2][0], sides[2 + n % 2][1])

    def parent_send(n, q):
        @pl.when(parent_out(n))
        def _():
            parent_copy(n, q).start()

    def parent_wait(offset, q):
        dx, dy = offset

        @pl.when(has(dx, dy))
        def _():
            pltpu.make_async_remote_copy(
                src_ref=zp.at[q],
                dst_ref=pgot.at[slot[offset], q],
                send_sem=send2.at[0, q],
                recv_sem=recv2.at[slot[offset], q],
                device_id=(ix + dx, iy + dy),
                device_id_type=MESH,
            ).wait_recv()

    def apply2(q, offsets):
        total = None
        for offset in offsets:
            term = dot(c2[0, 0, slot[offset]], pgot[slot[offset], q])
            total = term if total is None else total + term
        ptop[q] = ptop[q] - total

    def red2_out(q):
        return pltpu.make_async_copy(zp.at[q], red2_h.at[0, 0, :, pl.ds(q * w, w)], out2_sem.at[0, q])

    def skel2_out(q):
        return pltpu.make_async_copy(ptop.at[q], skel2_h.at[0, 0, :, pl.ds(q * w, w)], out2_sem.at[1, q])

    def solve2(q):
        tm = t2[0, 0]
        sk = ptop[q]
        diff = pred[q] - dot(tm, sk.astype(BF))
        zc = dot(p2[0, 0], diff.astype(BF)).astype(BF)
        zp[q] = zc
        for n in (2, 3, 0, 1):
            parent_send(n, q)
        red2_out(q).start()
        ptop[q] = sk - dot_t(tm, zc)

    LR = [(0, -1), (0, 1)]
    UD = [(-1, 0), (1, 0)]
    CN = [(-1, -1), (-1, 1), (1, -1), (1, 1)]

    def take(q, offsets):
        for offset in offsets:
            parent_wait(offset, q)
        apply2(q, offsets)

    def forward(q):
        for u in range(2):
            parent_wait(UD[u], q)
            parent_send(4 + 2 * u, q)
            parent_send(5 + 2 * u, q)

    role = 2 * lax.rem(ix, 2) + lax.rem(iy, 2)

    @pl.when(role == 0)
    def _():
        for q in qs:
            enter2(q)
            solve2(q)
        for q in qs:
            take(q, LR)
        for q in qs:
            forward(q)
        for q in qs:
            apply2(q, UD)
        for q in qs:
            take(q, CN)
            skel2_out(q).start()

    @pl.when(role == 1)
    def _():
        for q in qs:
            enter2(q)
        for q in qs:
            take(q, LR)
            solve2(q)
        for q in qs:
            take(q, CN)
        for q in qs:
            forward(q)
        for q in qs:
            apply2(q, UD)
            skel2_out(q).start()

    @pl.when(role == 2)
    def _():
        for q in qs:
            enter2(q)
        for q in qs:
            forward(q)
        for q in qs:
            apply2(q, UD)
        for q in qs:
            take(q, CN)
            solve2(q)
        for q in qs:
            take(q, LR)
            skel2_out(q).start()

    @pl.when(role == 3)
    def _():
        for q in qs:
            enter2(q)
        for q in qs:
            forward(q)
        for q in qs:
            apply2(q, UD)
        for q in qs:
            take(q, CN)
        for q in qs:
            take(q, LR)
            solve2(q)
            skel2_out(q).start()

    for q in qs:
        for color in range(4):
            red1_out(color, q).wait()
            for src in (ROW, COL, COR):
                @pl.when(leaf_out(color, src))
                def _(color=color, src=src, q=q):
                    leaf_copy(color, src, q).wait_send()
        for n in range(8):
            @pl.when(parent_out(n))
            def _(n=n, q=q):
                parent_copy(n, q).wait_send()
        red2_out(q).wait()
        skel2_out(q).wait()


def shards(rhs, perm1, interp1, pivinv1, couple1, perm2, interp2, pivinv2, couple2):
    r1, s1 = interp1.shape[-2:]
    r2, s2 = interp2.shape[-2:]
    k = rhs.shape[-1]
    w = 128 if k % 128 == 0 else k
    nq = k // w
    args = (rhs, perm1, interp1, pivinv1, couple1, perm2, interp2, pivinv2, couple2)
    anywhere = pl.BlockSpec(memory_space=pl.ANY)
    return pl.pallas_call(
        functools.partial(kernel, nq, w, s1, s2),
        out_shape=(
            jax.ShapeDtypeStruct((2, 2, r1, k), BF),
            jax.ShapeDtypeStruct((1, 1, r2, k), BF),
            jax.ShapeDtypeStruct((1, 1, s2, k), F32),
        ),
        in_specs=[anywhere] * len(args),
        out_specs=(anywhere,) * 3,
        scratch_shapes=[pltpu.VMEM(x.shape, x.dtype) for x in args]
        + [
            pltpu.VMEM((4, nq, s1, w), F32),
            pltpu.VMEM((4, nq, r1, w), F32),
            pltpu.VMEM((4, nq, r1, w), BF),
            pltpu.VMEM((4, 3, nq, r1, w), BF),
            pltpu.VMEM((nq, s2, w), F32),
            pltpu.VMEM((nq, r2, w), F32),
            pltpu.VMEM((nq, r2, w), BF),
            pltpu.VMEM((8, nq, r2, w), BF),
            pltpu.SemaphoreType.DMA((12,)),
            pltpu.SemaphoreType.DMA((4, nq)),
            pltpu.SemaphoreType.DMA((2, nq)),
            pltpu.SemaphoreType.DMA((4, 3, nq)),
            pltpu.SemaphoreType.DMA((4, 3, nq)),
            pltpu.SemaphoreType.DMA((8, nq)),
            pltpu.SemaphoreType.DMA((8, nq)),
        ],
        compiler_params=pltpu.CompilerParams(
            collective_id=0, has_side_effects=True, vmem_limit_bytes=40 * 1024 * 1024
        ),
        name="eliminate",
    )(*args)


def solution(mesh):
    in_specs = (
        P("bx", "by", None, None),
        P("bx", "by", None),
        P("bx", "by", None, None),
        P("bx", "by", None, None),
        P("bx", "by", None, None, None),
        P("bx", "by", None),
        P("bx", "by", None, None),
        P("bx", "by", None, None),
        P("bx", "by", None, None, None),
    )
    out_specs = (P("bx", "by", None, None), P("bx", "by", None, None), P("bx", "by", None, None))
    return jax.shard_map(shards, mesh=mesh, in_specs=in_specs, out_specs=out_specs, check_vma=False)
```

```python
import functools

import jax
import jax.numpy as jnp
from jax import lax
from jax.experimental import pallas as pl
from jax.experimental.pallas import tpu as pltpu
from jax.sharding import PartitionSpec as P

OFFSETS = [(-1, -1), (-1, 0), (-1, 1), (0, -1), (0, 1), (1, -1), (1, 0), (1, 1)]
BF = jnp.bfloat16
F32 = jnp.float32
MESH = pl.DeviceIdType.MESH
OWN, ROW, COL, COR = 0, 1, 2, 3
LR = [(0, -1), (0, 1)]
UD = [(-1, 0), (1, 0)]


def dot(a, b):
    return jnp.dot(a, b, preferred_element_type=F32)


def dot_t(a, b):
    return lax.dot_general(a, b, (((0,), (0,)), ((), ())), preferred_element_type=F32)


def sources():
    table = []
    for color in range(4):
        a, b = color // 2, color % 2
        per_box = []
        for box in range(4):
            nx, ny = box // 2, box % 2
            found = []
            if box != color:
                for k, (dx, dy) in enumerate(OFFSETS):
                    r, c = nx + dx, ny + dy
                    if r % 2 == a and c % 2 == b:
                        row_in, col_in = 0 <= r <= 1, 0 <= c <= 1
                        if row_in and col_in:
                            src = OWN
                        elif col_in:
                            src = ROW
                        elif row_in:
                            src = COL
                        else:
                            src = COR
                        found.append((src, k))
            per_box.append(found)
        table.append(per_box)
    return table


TABLE = sources()


def reorder(perm_row, values):
    n = values.shape[0]
    hit = lax.broadcasted_iota(jnp.int32, (n, n), 0) == perm_row
    onehot = jnp.where(hit, 1.0, 0.0).astype(BF)
    high = values.astype(BF)
    low = (values - high.astype(F32)).astype(BF)
    both = dot_t(onehot, jnp.concatenate([high, low], axis=1))
    w = values.shape[1]
    return both[:, :w] + both[:, w:]


def kernel(
    nq, w, s1, s2,
    rhs_h, perm1_h, t1_h, p1_h, c1_h, perm2_h, t2_h, p2_h, c2_h,
    red1_h, red2_h, skel2_h,
    rhs, perm1, t1, p1, c1t, perm2, t2, p2, c2,
    skel, red, zb, got, ptop, pred, zp, pz, po, pu, cf,
    in_sem, out1_sem, out2_sem, send1, recv1, sendc, recvc, sendz, recvz, sendu, recvu,
):
    nx, ny = lax.axis_size("bx"), lax.axis_size("by")
    ix, iy = lax.axis_index("bx"), lax.axis_index("by")

    def has(dx, dy):
        cond = None
        for d, i, n in ((dx, ix, nx), (dy, iy, ny)):
            if d:
                here = (i > 0) if d < 0 else (i < n - 1)
                cond = here if cond is None else jnp.logical_and(cond, here)
        return cond

    def load(n, src, dst):
        return pltpu.make_async_copy(src, dst, in_sem.at[n])

    rhs_in = [load(i, rhs_h.at[i // 2, i % 2], rhs.at[i // 2, i % 2]) for i in range(4)]
    rest = [
        load(4 + i, s, d)
        for i, (s, d) in enumerate(
            [(perm1_h, perm1), (t1_h, t1), (p1_h, p1), (c1_h, c1t), (perm2_h, perm2), (t2_h, t2), (p2_h, p2), (c2_h, c2)]
        )
    ]
    perm1_in, t1_in, p1_in, c1_in, perm2_in, t2_in, p2_in, c2_in = rest
    for copy in [perm1_in, rhs_in[0], t1_in, p1_in, rhs_in[1], c1_in, rhs_in[2], rhs_in[3], perm2_in, t2_in, p2_in, c2_in]:
        copy.start()

    barrier = pltpu.get_barrier_semaphore()
    sides = [(-1, 0), (1, 0), (0, -1), (0, 1)]
    for dx, dy in sides:
        @pl.when(has(dx, dy))
        def _(dx=dx, dy=dy):
            pl.semaphore_signal(barrier, inc=1, device_id=(ix + dx, iy + dy), device_id_type=MESH)

    for color in range(4):
        sx = 1 if color // 2 else -1
        sy = 1 if color % 2 else -1
        for src, (dx, dy) in ((ROW, (-sx, 0)), (COL, (0, -sy)), (COR, (-sx, -sy))):
            @pl.when(jnp.logical_not(has(dx, dy)))
            def _(color=color, src=src):
                got[color, src - 1] = jnp.zeros(got.shape[2:], BF)
    for n in range(2):
        @pl.when(jnp.logical_not(has(*LR[n])))
        def _(n=n):
            pz[n] = jnp.zeros(pz.shape[1:], BF)

        @pl.when(jnp.logical_not(has(*UD[n])))
        def _(n=n):
            for kind in range(2):
                pu[kind, n] = jnp.zeros(pu.shape[2:], BF)

    def couple_copy(u):
        return pltpu.make_async_remote_copy(
            src_ref=c2_h.at[0, 0, pl.ds(5 * u, 3)],
            dst_ref=cf.at[1 - u],
            send_sem=sendc.at[u],
            recv_sem=recvc.at[1 - u],
            device_id=(ix + UD[u][0], iy),
            device_id_type=MESH,
        )

    def unpack(box):
        i, j = box // 2, box % 2
        values = reorder(perm1[i, pl.ds(j, 1), :], rhs[i, j])
        for q in range(nq):
            part = values[:, q * w:(q + 1) * w]
            skel[box, q] = part[:s1]
            red[box, q] = part[s1:]

    perm1_in.wait()
    rhs_in[0].wait()
    unpack(0)
    t1_in.wait()
    p1_in.wait()

    peers = sum(jnp.where(has(dx, dy), 1, 0) for dx, dy in sides)
    pl.semaphore_wait(barrier, peers)

    def leaf_copy(color, src, q):
        sx = 1 if color // 2 else -1
        sy = 1 if color % 2 else -1
        if src == ROW:
            block, to = zb.at[color, q], (ix + sx, iy)
        elif src == COL:
            block, to = zb.at[color, q], (ix, iy + sy)
        else:
            block, to = got.at[color, ROW - 1, q], (ix, iy + sy)
        return pltpu.make_async_remote_copy(
            src_ref=block,
            dst_ref=got.at[color, src - 1, q],
            send_sem=send1.at[color, src - 1, q],
            recv_sem=recv1.at[color, src - 1, q],
            device_id=to,
            device_id_type=MESH,
        )

    def leaf_out(color, src):
        sx = 1 if color // 2 else -1
        sy = 1 if color % 2 else -1
        if src == ROW:
            return has(sx, 0)
        if src == COL:
            return has(0, sy)
        return jnp.logical_and(has(-sx, 0), has(0, sy))

    def leaf_in(color, src):
        sx = 1 if color // 2 else -1
        sy = 1 if color % 2 else -1
        return has(*{ROW: (-sx, 0), COL: (0, -sy), COR: (-sx, -sy)}[src])

    def leaf_send(color, src, q):
        @pl.when(leaf_out(color, src))
        def _():
            leaf_copy(color, src, q).start()

    def leaf_wait(color, src, q):
        @pl.when(leaf_in(color, src))
        def _():
            leaf_copy(color, src, q).wait_recv()

    def leaf_forward(color, q):
        leaf_wait(color, ROW, q)
        leaf_send(color, COR, q)

    def red1_out(color, q):
        a, b = color // 2, color % 2
        return pltpu.make_async_copy(zb.at[color, q], red1_h.at[a, b, :, pl.ds(q * w, w)], out1_sem.at[color, q])

    def solve1(box, q):
        a, b = box // 2, box % 2
        tm = t1[a, b]
        sk = skel[box, q]
        diff = red[box, q] - dot(tm, sk.astype(BF))
        zc = dot(p1[a, b], diff.astype(BF)).astype(BF)
        zb[box, q] = zc
        leaf_send(box, COL, q)
        leaf_send(box, ROW, q)
        red1_out(box, q).start()
        skel[box, q] = sk - dot_t(tm, zc)

    def apply1(box, q, *which):
        total = None
        for color, src in which:
            for s, k in TABLE[color][box]:
                if s == src:
                    z = zb[color, q] if s == OWN else got[color, s - 1, q]
                    term = dot_t(c1t[box // 2, box % 2, k], z)
                    total = term if total is None else total + term
        skel[box, q] = skel[box, q] - total

    qs = range(nq)
    for q in qs:
        solve1(0, q)
    @pl.when(has(*UD[1]))
    def _():
        couple_copy(1).start()

    rhs_in[1].wait()
    unpack(1)
    c1_in.wait()

    for q in qs:
        apply1(1, q, (0, OWN))
    for q in qs:
        leaf_wait(0, COL, q)
        apply1(1, q, (0, COL))
        solve1(1, q)
    for box in (2, 3):
        rhs_in[box].wait()
        unpack(box)
    for q in qs:
        leaf_forward(0, q)
    for q in qs:
        apply1(2, q, (0, OWN), (0, ROW), (1, OWN))
    for q in qs:
        leaf_forward(1, q)
    for q in qs:
        leaf_wait(1, COL, q)
        apply1(2, q, (1, ROW), (1, COL))
    for q in qs:
        leaf_wait(1, COR, q)
        apply1(2, q, (1, COR))
        solve1(2, q)

    @pl.when(has(*UD[0]))
    def _():
        couple_copy(0).start()

    for q in qs:
        leaf_wait(0, COR, q)
        apply1(3, q, (0, OWN), (0, ROW), (0, COL), (0, COR), (1, OWN), (1, ROW), (2, OWN))
    for q in qs:
        leaf_wait(2, COL, q)
        apply1(3, q, (2, COL))
        solve1(3, q)
    for q in qs:
        leaf_forward(2, q)
    for q in qs:
        apply1(0, q, (1, OWN), (1, COL), (2, OWN), (2, ROW), (3, OWN))
        apply1(1, q, (2, OWN), (2, ROW), (2, COL), (3, OWN))
        apply1(2, q, (3, OWN))
    for q in qs:
        leaf_forward(3, q)
    for q in qs:
        leaf_wait(2, COR, q)
        leaf_wait(3, COL, q)
        apply1(0, q, (3, ROW), (3, COL))
        apply1(1, q, (2, COR), (3, ROW))
        apply1(2, q, (3, COL))

    perm2_in.wait()
    order2 = perm2[0]
    t2_in.wait()
    p2_in.wait()
    c2_in.wait()

    def enter2(q):
        leaf_wait(3, COR, q)
        apply1(0, q, (3, COR))
        children = jnp.concatenate([skel[box, q] for box in range(4)], axis=0)
        values = reorder(order2, children)
        ptop[q] = values[:s2]
        pred[q] = values[s2:]

    for u in range(2):
        @pl.when(has(*UD[u]))
        def _(u=u):
            couple_copy(1 - u).wait_recv()

    def side_copy(n, q):
        return pltpu.make_async_remote_copy(
            src_ref=zp.at[q],
            dst_ref=pz.at[1 - n, q],
            send_sem=sendz.at[n, q],
            recv_sem=recvz.at[1 - n, q],
            device_id=(ix, iy + LR[n][1]),
            device_id_type=MESH,
        )

    def product_copy(kind, u, q):
        return pltpu.make_async_remote_copy(
            src_ref=po.at[kind, u, q],
            dst_ref=pu.at[kind, 1 - u, q],
            send_sem=sendu.at[kind, u, q],
            recv_sem=recvu.at[kind, 1 - u, q],
            device_id=(ix + UD[u][0], iy),
            device_id_type=MESH,
        )

    def red2_out(q):
        return pltpu.make_async_copy(zp.at[q], red2_h.at[0, 0, :, pl.ds(q * w, w)], out2_sem.at[0, q])

    def skel2_out(q):
        return pltpu.make_async_copy(ptop.at[q], skel2_h.at[0, 0, :, pl.ds(q * w, w)], out2_sem.at[1, q])

    def solve2(q):
        tm = t2[0, 0]
        sk = ptop[q]
        diff = pred[q] - dot(tm, sk.astype(BF))
        zc = dot(p2[0, 0], diff.astype(BF)).astype(BF)
        zp[q] = zc
        for n in range(2):
            @pl.when(has(*LR[n]))
            def _(n=n):
                side_copy(n, q).start()
        red2_out(q).start()
        for u in range(2):
            @pl.when(has(*UD[u]))
            def _(u=u):
                po[0, u, q] = dot(cf[u, 1], zp[q]).astype(BF)
                product_copy(0, u, q).start()
        ptop[q] = sk - dot_t(tm, zc)

    def wait_lr(q):
        for n in range(2):
            @pl.when(has(*LR[n]))
            def _(n=n):
                side_copy(1 - n, q).wait_recv()

    def apply_lr(q):
        ptop[q] = ptop[q] - (dot(c2[0, 0, 3], pz[0, q]) + dot(c2[0, 0, 4], pz[1, q]))

    def relay(q):
        for u in range(2):
            @pl.when(has(*UD[u]))
            def _(u=u):
                both = dot(cf[u, 0], pz[0, q]) + dot(cf[u, 2], pz[1, q])
                po[1, u, q] = both.astype(BF)
                product_copy(1, u, q).start()

    def take(kind, q):
        for u in range(2):
            @pl.when(has(*UD[u]))
            def _(u=u):
                product_copy(kind, 1 - u, q).wait_recv()
        ptop[q] = ptop[q] - (pu[kind, 0, q].astype(F32) + pu[kind, 1, q].astype(F32))

    role = 2 * lax.rem(ix, 2) + lax.rem(iy, 2)

    @pl.when(role == 0)
    def _():
        for q in qs:
            enter2(q)
            solve2(q)
        for q in qs:
            wait_lr(q)
            relay(q)
        for q in qs:
            apply_lr(q)
        for q in qs:
            take(0, q)
        for q in qs:
            take(1, q)
            skel2_out(q).start()

    @pl.when(role == 1)
    def _():
        for q in qs:
            enter2(q)
        for q in qs:
            wait_lr(q)
            apply_lr(q)
            solve2(q)
        for q in qs:
            relay(q)
        for q in qs:
            take(1, q)
        for q in qs:
            take(0, q)
            skel2_out(q).start()

    @pl.when(role == 2)
    def _():
        for q in qs:
            enter2(q)
        for q in qs:
            take(0, q)
        for q in qs:
            take(1, q)
            solve2(q)
        for q in qs:
            wait_lr(q)
            relay(q)
        for q in qs:
            apply_lr(q)
            skel2_out(q).start()

    @pl.when(role == 3)
    def _():
        for q in qs:
            enter2(q)
        for q in qs:
            take(0, q)
        for q in qs:
            take(1, q)
        for q in qs:
            wait_lr(q)
            apply_lr(q)
            solve2(q)
        for q in qs:
            skel2_out(q).start()
            relay(q)

    for q in qs:
        for color in range(4):
            red1_out(color, q).wait()
            for src in (ROW, COL, COR):
                @pl.when(leaf_out(color, src))
                def _(color=color, src=src, q=q):
                    leaf_copy(color, src, q).wait_send()
        for n in range(2):
            @pl.when(has(*LR[n]))
            def _(n=n, q=q):
                side_copy(n, q).wait_send()

            @pl.when(has(*UD[n]))
            def _(n=n, q=q):
                product_copy(0, n, q).wait_send()
                product_copy(1, n, q).wait_send()
        red2_out(q).wait()
        skel2_out(q).wait()
    for u in range(2):
        @pl.when(has(*UD[u]))
        def _(u=u):
            couple_copy(u).wait_send()


def deliver(*refs):
    sources, targets, held, sem = refs[:3], refs[3:6], refs[6:9], refs[9]
    inward, outward = [], []
    for src, mid, dst in zip(sources, held, targets):
        for i in range(src.shape[0]):
            for j in range(src.shape[1]):
                n = len(inward)
                inward.append(pltpu.make_async_copy(src.at[i, j], mid.at[i, j], sem.at[0, n]))
                outward.append(pltpu.make_async_copy(mid.at[i, j], dst.at[i, j], sem.at[1, n]))
    for copy in inward:
        copy.start()
    for first, second in zip(inward, outward):
        first.wait()
        second.start()
    for copy in outward:
        copy.wait()


def shards(rhs, perm1, interp1, pivinv1, couple1, perm2, interp2, pivinv2, couple2):
    r1, s1 = interp1.shape[-2:]
    r2, s2 = interp2.shape[-2:]
    k = rhs.shape[-1]
    w = 128 if k % 128 == 0 else k
    nq = k // w
    couple1 = jnp.swapaxes(couple1, -1, -2)
    args = (rhs, perm1, interp1, pivinv1, couple1, perm2, interp2, pivinv2, couple2)
    anywhere = pl.BlockSpec(memory_space=pl.ANY)
    far = pl.BlockSpec(memory_space=pltpu.HBM)
    outs = pl.pallas_call(
        functools.partial(kernel, nq, w, s1, s2),
        out_shape=(
            jax.ShapeDtypeStruct((2, 2, r1, k), BF),
            jax.ShapeDtypeStruct((1, 1, r2, k), BF),
            jax.ShapeDtypeStruct((1, 1, s2, k), F32),
        ),
        in_specs=[far] * len(args),
        out_specs=(anywhere,) * 3,
        scratch_shapes=[pltpu.VMEM(x.shape, x.dtype) for x in args]
        + [
            pltpu.VMEM((4, nq, s1, w), F32),
            pltpu.VMEM((4, nq, r1, w), F32),
            pltpu.VMEM((4, nq, r1, w), BF),
            pltpu.VMEM((4, 3, nq, r1, w), BF),
            pltpu.VMEM((nq, s2, w), F32),
            pltpu.VMEM((nq, r2, w), F32),
            pltpu.VMEM((nq, r2, w), BF),
            pltpu.VMEM((2, nq, r2, w), BF),
            pltpu.VMEM((2, 2, nq, s2, w), BF),
            pltpu.VMEM((2, 2, nq, s2, w), BF),
            pltpu.VMEM((2, 3, s2, r2), BF),
            pltpu.SemaphoreType.DMA((12,)),
            pltpu.SemaphoreType.DMA((4, nq)),
            pltpu.SemaphoreType.DMA((2, nq)),
            pltpu.SemaphoreType.DMA((4, 3, nq)),
            pltpu.SemaphoreType.DMA((4, 3, nq)),
            pltpu.SemaphoreType.DMA((2,)),
            pltpu.SemaphoreType.DMA((2,)),
            pltpu.SemaphoreType.DMA((2, nq)),
            pltpu.SemaphoreType.DMA((2, nq)),
            pltpu.SemaphoreType.DMA((2, 2, nq)),
            pltpu.SemaphoreType.DMA((2, 2, nq)),
        ],
        compiler_params=pltpu.CompilerParams(
            collective_id=0, has_side_effects=True, vmem_limit_bytes=60 * 1024 * 1024
        ),
        name="eliminate",
    )(*args)
    return pl.pallas_call(
        deliver,
        out_shape=tuple(jax.ShapeDtypeStruct(x.shape, x.dtype) for x in outs),
        in_specs=[anywhere] * 3,
        out_specs=(anywhere,) * 3,
        scratch_shapes=[pltpu.VMEM(x.shape, x.dtype) for x in outs] + [pltpu.SemaphoreType.DMA((2, 8))],
        compiler_params=pltpu.CompilerParams(vmem_limit_bytes=60 * 1024 * 1024),
        name="deliver",
    )(*outs)


def solution(mesh):
    in_specs = (
        P("bx", "by", None, None),
        P("bx", "by", None),
        P("bx", "by", None, None),
        P("bx", "by", None, None),
        P("bx", "by", None, None, None),
        P("bx", "by", None),
        P("bx", "by", None, None),
        P("bx", "by", None, None),
        P("bx", "by", None, None, None),
    )
    out_specs = (P("bx", "by", None, None), P("bx", "by", None, None), P("bx", "by", None, None))
    return jax.shard_map(shards, mesh=mesh, in_specs=in_specs, out_specs=out_specs, check_vma=False)
```
